768 devices in a mesh: dp: 32 (over x, y), ctx: 24 (over z, core).
Axes of the slice: x: 4, y: 8, z: 12, core: 2. Of those that a mesh axis runs over, the one named last changes fastest.
Arguments:
- tokens: bfloat16 [6144, 5120], P('dp'), may hold values from -6 to 6
- scores: float32 [6144, 8], P('dp'), may hold values from -12 to 12
- routes: int32 [6144, 1], P('dp'), may hold values from 0 to 127; in each aligned block of 192 rows (0 to 191, 192 to 383, ...) at most 4 rows name the same one
- w_gate: bfloat16 [5120, 98304], P(None, ('dp', 'ctx')), may hold values from -0.078125 to 0.078125
- w_up: bfloat16 [5120, 98304], P(None, ('dp', 'ctx')), may hold values from -0.078125 to 0.078125
- w_down: bfloat16 [98304, 5120], P(('dp', 'ctx')), may hold values from -0.21875 to 0.21875
Outputs:
- mixed: bfloat16 [6144, 5120], P(('dp', 'ctx'))
The draws below stay inside these ranges and needn't reach their ends.
Inputs may be any that keep to these rules, and one draw needn't show every extreme that they name: Within each aligned block of 192 tokens (the tokens of one index of dp), a token's 1 routes name different experts, no expert is named more than 4 times in the block, a bound that some block reaches.
All inputs are finite; a program needn't handle non-finite values.
Results may differ from the reference program's by a relative error of at most 0.006.
Values may be sent and summed in bfloat16 or wider, within the bound.
No kernel may reach another device: no remote copies, remote signals or barrier semaphores. Data moves between devices by JAX's collectives and lax.ppermute only.
A program may use at most 32 MiB of HBM per device.

```python
import math
import jax
import jax.numpy as jnp
import numpy as np
from jax import lax

D = 5120
TOP = 8
FF = 768
K_FLY = 1
EXP_DP = 4
CAP = 4
EXPERTS = 128
TOK_DP = 192
TOKENS = 6144
N_DP = 32
N_CTX = 24


def block_levels(own_key, dims, pieces, smallest, largest):
    def one(axis_at, blocks):
        draws = jax.random.uniform(jax.random.fold_in(jax.random.fold_in(own_key, 6), axis_at), (blocks,), jnp.float32, smallest / len(pieces), largest / len(pieces))
        return jnp.repeat(jnp.exp(draws), dims[axis_at] // blocks).reshape((-1,) + (1,) * (len(dims) - axis_at - 1))

    gain = one(*pieces[0])
    for cut in pieces[1:]:
        gain = gain * one(*cut)
    return gain


def routed_block(own_key, own, number, rows, number_of, top, limit, slope):
    ranking = jax.random.permutation(own_key, number_of)
    heavy_load, common = load_shares(number_of, rows * top, limit, slope, True), load_shares(number_of, rows * top, limit, slope, False)
    places = jnp.arange(number_of)

    def named(tallies, rotation):
        used = int((tallies > 0).sum())
        fixed = max(1, used // 4)
        shifted = fixed + (places - fixed + rotation * (used - fixed)) % max(1, number_of - fixed)
        return jnp.zeros((number_of,), jnp.int32).at[ranking[jnp.where(places < fixed, places, shifted)]].set(jnp.asarray(tallies, jnp.int32))

    tallies = jnp.where(number % 4 == 0, named(heavy_load, number // 4), named(common, number - number // 4 - 1))
    mixed = jax.random.permutation(jax.random.fold_in(own, 3), number_of)
    donor, taker = mixed[0:number_of // 2 * 2:2], mixed[1:number_of // 2 * 2:2]
    margin = jnp.minimum(tallies[donor] - 1, limit - tallies[taker]) // 2
    margin = jnp.where((donor == ranking[0]) | (taker == ranking[0]) | (tallies[taker] == 0), 0, jnp.maximum(margin, 0))
    shifted = jax.random.randint(jax.random.fold_in(own, 4), (number_of // 2,), 0, 1 << 20) % (margin + 1)
    tallies = tallies.at[donor].add(-shifted).at[taker].add(shifted)
    items = jnp.searchsorted(jnp.cumsum(tallies), jnp.arange(rows * top), side="right").astype(jnp.int32)
    listing = items.reshape(top, rows).T
    listing = listing[jax.random.permutation(jax.random.fold_in(own, 1), rows)]
    rotation = jax.random.randint(jax.random.fold_in(own, 2), (rows, 1), 0, top)
    return jnp.take_along_axis(listing, (jnp.arange(top)[None, :] + rotation) % top, axis=1)


def load_shares(count, total, limit, slope, full):
    portions = [(1 << 20) // math.isqrt(grade ** slope) + 1 for grade in range(1, count + 1)]
    largest = limit if full else min(limit, max(-(-total // count), total * portions[0] // sum(portions)))
    least = 1 if total - largest >= count - 1 else 0
    counts, spare = [largest] + [least] * (count - 1), total - largest - least * (count - 1)
    while spare > 0:
        candidates = [i for i in range(1, count) if counts[i] < largest] or [i for i in range(1, count) if counts[i] < limit]
        mass, left = sum([portions[i] for i in candidates]), spare
        for i in candidates:
            addition = min(limit - counts[i], max(1, left * portions[i] // mass), spare)
            counts[i] = counts[i] + addition
            spare = spare - addition
    return np.array(counts)


def normal_values(rng, shape, spread, reach, pieces=(), kind=jnp.bfloat16):
    drawn = jax.random.normal(rng, shape, jnp.float32) * spread
    if len(pieces) > 0:
        drawn = block_levels(rng, shape, pieces, -0.22, 0.18) * drawn
    return jnp.clip(drawn, min=-reach, max=reach).astype(kind)


def setup_inputs(seed: int = 0) -> dict:
    keys = jax.random.split(jax.random.key(seed), 7)
    tokens = normal_values(keys[0], (TOKENS, D), 1.0, 6.0, ((0, 32),))
    scores = normal_values(keys[1], (TOKENS, TOP), 2.0, 12.0, ((0, 32),), jnp.float32)
    routes_keys = jax.random.split(jax.random.fold_in(keys[2], 1), TOKENS // TOK_DP)
    routes_turns = jax.random.permutation(jax.random.fold_in(keys[2], 3), TOKENS // TOK_DP)
    routes = jax.vmap(lambda own, number: routed_block(jax.random.fold_in(keys[2], 2), own, number, TOK_DP, EXPERTS, K_FLY, CAP, 2))(routes_keys, routes_turns).reshape((TOKENS, K_FLY))
    w_gate = normal_values(keys[3], (D, EXPERTS * FF), D ** -0.5, 0.078125, ((1, 768),))
    w_up = normal_values(keys[4], (D, EXPERTS * FF), D ** -0.5, 0.078125, ((1, 768),))
    w_down = normal_values(keys[5], (EXPERTS * FF, D), FF ** -0.5, 0.21875, ((0, 768),))
    return {"tokens": tokens, "scores": scores, "routes": routes, "w_gate": w_gate, "w_up": w_up, "w_down": w_down}


route_scale = 2.5


def reference(tokens, scores, routes, w_gate, w_up, w_down):
    parts = N_CTX // EXP_DP
    width = FF // parts
    per_block = TOK_DP * K_FLY
    sig = jax.nn.sigmoid(scores)
    gates = route_scale * sig[:, :K_FLY] / jnp.sum(sig, axis=1, keepdims=True)
    grouped = routes.reshape(N_DP, per_block)
    onehot = (grouped[:, :, None] == jnp.arange(EXPERTS, dtype=jnp.int32)[None, None, :]).astype(jnp.int32)
    before = (jnp.cumsum(onehot, axis=1) - onehot).astype(jnp.int32)
    slot = jnp.sum(before * onehot, axis=2).astype(jnp.int32)
    route_ids = jnp.arange(N_DP * per_block, dtype=jnp.int32).reshape(N_DP, per_block)
    source = jnp.broadcast_to(jnp.arange(N_DP, dtype=jnp.int32)[:, None], grouped.shape)
    table = jnp.full((EXPERTS, N_DP, CAP), TOKENS * K_FLY, jnp.int32)
    table = table.at[grouped, source, slot].set(route_ids)
    padded = jnp.concatenate([tokens, jnp.zeros((1, D), jnp.bfloat16)], axis=0)
    flat_gates = jnp.concatenate([gates.reshape(-1), jnp.zeros((1,), jnp.float32)])

    def one_expert(total, expert):
        ids = table[expert].reshape(-1)
        owners = (ids // K_FLY).astype(jnp.int32)
        rows = padded[owners]
        start = (expert * FF).astype(jnp.int32)
        gate_cols = lax.dynamic_slice_in_dim(w_gate, start, FF, 1)
        up_cols = lax.dynamic_slice_in_dim(w_up, start, FF, 1)
        down_rows = lax.dynamic_slice_in_dim(w_down, start, FF, 0)
        pre_gate = jnp.dot(rows, gate_cols, preferred_element_type=jnp.float32)
        pre_up = jnp.dot(rows, up_cols, preferred_element_type=jnp.float32)
        hidden = (jax.nn.silu(pre_gate) * pre_up).astype(jnp.bfloat16)
        summed = jnp.zeros((rows.shape[0], D), jnp.float32)
        for part in range(parts):
            piece = jnp.dot(hidden[:, part * width:(part + 1) * width], down_rows[part * width:(part + 1) * width], preferred_element_type=jnp.float32).astype(jnp.bfloat16)
            summed = summed + piece.astype(jnp.float32)
        weighted = summed * flat_gates[ids][:, None]
        return total.at[owners].add(weighted), None

    total, _ = lax.scan(one_expert, jnp.zeros((TOKENS + 1, D), jnp.float32), jnp.arange(EXPERTS, dtype=jnp.int32))
    return total[:TOKENS].astype(jnp.bfloat16)
```

```python
import functools

import jax
import jax.numpy as jnp
from jax import lax
from jax.experimental import pallas as pl
from jax.experimental.pallas import tpu as pltpu
from jax.sharding import Mesh
from jax.sharding import PartitionSpec as P

EXP_DP = 4
CAP = 4
CORES = 2
LANES = 128
ROUTE_SCALE = 2.5
VMEM_LIMIT = 48 * 1024 * 1024

VMEM = pl.BlockSpec(memory_space=pltpu.VMEM)
SMEM = pl.BlockSpec(memory_space=pltpu.SMEM)
PARAMS = pltpu.CompilerParams(vmem_limit_bytes=VMEM_LIMIT)


def slot_of_tokens(routes, group):
    tokens = routes.shape[0]
    row = lax.broadcasted_iota(jnp.int32, (tokens, tokens), 0)
    col = lax.broadcasted_iota(jnp.int32, (tokens, tokens), 1)
    across = jnp.broadcast_to(routes, (tokens, tokens))
    flat = jnp.sum(jnp.where(row == col, across, 0), axis=0, keepdims=True)
    same = (across == flat) & (row < col)
    rank = jnp.sum(same.astype(jnp.int32), axis=0, keepdims=True)
    slot = (flat >> 2) * CAP + rank
    return jnp.where((flat & 3) == group, slot, jnp.int32(1 << 20))


def pick_kernel(place_ref, routes_ref, tokens_ref, out_ref):
    slots, width = out_ref.shape
    tokens = routes_ref.shape[0]
    slot = slot_of_tokens(routes_ref[...], place_ref[0])
    rows = lax.broadcasted_iota(jnp.int32, (slots, tokens), 0)
    pick = jnp.where(rows == slot, 1.0, 0.0).astype(jnp.bfloat16)
    start = pl.multiple_of(place_ref[2] * width, LANES)
    out_ref[...] = jnp.dot(
        pick, tokens_ref[:, pl.ds(start, width)], preferred_element_type=jnp.float32
    ).astype(jnp.bfloat16)


def hidden_kernel(place_ref, own_ref, other_ref, gate_ref, up_ref, out_ref):
    half = own_ref.shape[1]
    mine = pl.multiple_of(place_ref[2] * half, LANES)
    theirs = pl.multiple_of((1 - place_ref[2]) * half, LANES)

    def project(w_ref):
        return jnp.dot(
            own_ref[...], w_ref[pl.ds(mine, half), :], preferred_element_type=jnp.float32
        ) + jnp.dot(
            other_ref[...], w_ref[pl.ds(theirs, half), :], preferred_element_type=jnp.float32
        )

    pre_gate = project(gate_ref)
    pre_up = project(up_ref)
    out_ref[...] = (pre_gate * jax.nn.sigmoid(pre_gate) * pre_up).astype(jnp.bfloat16)


def down_kernel(place_ref, hidden_ref, own_ref, next_ref, last_ref, swap_ref, out_ref):
    rows, width = out_ref.shape
    third = place_ref[1]
    core = place_ref[2]
    base = jnp.minimum(third * (2 * width), own_ref.shape[1] - 2 * width)
    here = pl.multiple_of(base + core * width, LANES)
    local = pl.multiple_of(core * width, LANES)
    total = jnp.zeros((rows, width), jnp.float32)
    for step in range(3):
        source = lax.rem(third + 3 - step, 3)
        if step == 0:
            weights = own_ref[:, pl.ds(here, width)]
        else:
            weights = (next_ref, last_ref)[step - 1][:, pl.ds(local, width)]
        total += jnp.dot(
            hidden_ref[2 * source + core], weights, preferred_element_type=jnp.float32
        )
        total += jnp.dot(
            hidden_ref[2 * source + 1 - core],
            swap_ref[step],
            preferred_element_type=jnp.float32,
        )
    out_ref[...] = total.astype(jnp.bfloat16)


def spread_kernel(place_ref, routes_ref, back_ref, out_ref):
    slots = back_ref.shape[0]
    tokens = out_ref.shape[0]
    slot = slot_of_tokens(routes_ref[...], place_ref[0])
    rows = lax.broadcasted_iota(jnp.int32, (slots, tokens), 0)
    pick = jnp.where(rows == slot, 1.0, 0.0).astype(jnp.bfloat16)
    out_ref[...] = lax.dot_general(
        pick, back_ref[...], (((0,), (0,)), ((), ())), preferred_element_type=jnp.float32
    ).astype(jnp.bfloat16)


def finish_kernel(place_ref, scores_ref, parts_ref, out_ref):
    rows, model = out_ref.shape
    width = parts_ref.shape[1]
    start = pl.multiple_of(place_ref[3] * rows, rows)
    sig = jax.nn.sigmoid(scores_ref[pl.ds(start, rows), :])
    gates = ROUTE_SCALE * sig[:, :1] / jnp.sum(sig, axis=1, keepdims=True)
    parts = parts_ref[...].astype(jnp.float32)
    per_group = parts.shape[0] // EXP_DP
    total = parts[:per_group]
    for group in range(1, EXP_DP):
        total = total + parts[group * per_group : (group + 1) * per_group]
    count = per_group // rows
    for part in range(count):
        third, core = part // CORES, part % CORES
        base = min(third * CORES * width, model - CORES * width) + core * width
        skip = max(0, third * CORES * width + core * width - base) if core == 0 else 0
        block = total[part * rows : (part + 1) * rows]
        out_ref[:, base + skip : base + width] = (block[:, skip:] * gates).astype(jnp.bfloat16)


def per_device(tokens, scores, routes, w_gate, w_up, w_down):
    dp_count = lax.axis_size("dp")
    model = tokens.shape[1]
    tok_rows = tokens.shape[0]
    hidden_units = w_down.shape[0]
    thirds = lax.axis_size("j")
    parts = thirds * CORES
    owners = EXP_DP * parts
    slots = dp_count * CAP
    half = model // CORES
    width = -(-model // (parts * LANES)) * LANES
    group, third, core = lax.axis_index("g"), lax.axis_index("j"), lax.axis_index("k")
    owner = (group * thirds + third) * CORES + core
    place = jnp.stack([group, third, core, owner]).astype(jnp.int32)
    bf = jnp.bfloat16

    def columns(to):
        start = jnp.minimum(to * (CORES * width), model - CORES * width)
        return lax.dynamic_slice_in_dim(w_down, start, CORES * width, 1)

    moved = []
    for step in (1, 2):
        moved.append(
            lax.ppermute(
                columns(lax.rem(third + step, thirds)),
                "j",
                [(i, (i + step) % thirds) for i in range(thirds)],
            )
        )
    mine_down = columns(third)
    away = (1 - core) * width
    swap = jnp.stack(
        [lax.dynamic_slice_in_dim(w, away, width, 1) for w in (mine_down, moved[0], moved[1])]
    )
    swapped = lax.ppermute(swap, "k", [(0, 1), (1, 0)])

    outgoing = pl.pallas_call(
        pick_kernel,
        out_shape=jax.ShapeDtypeStruct((slots, half), bf),
        in_specs=[SMEM, VMEM, VMEM],
        out_specs=VMEM,
        compiler_params=PARAMS,
    )(place, routes, tokens)
    arrived = lax.all_to_all(
        outgoing.reshape(dp_count, CAP, half), "dp", split_axis=0, concat_axis=0, tiled=True
    )
    other = lax.ppermute(arrived, "k", [(0, 1), (1, 0)])
    hidden = pl.pallas_call(
        hidden_kernel,
        out_shape=jax.ShapeDtypeStruct((slots, hidden_units), bf),
        in_specs=[SMEM] + [VMEM] * 4,
        out_specs=VMEM,
        compiler_params=PARAMS,
    )(place, arrived.reshape(slots, half), other.reshape(slots, half), w_gate, w_up)
    all_hidden = lax.all_gather(hidden, ("j", "k"), axis=0)
    piece = pl.pallas_call(
        down_kernel,
        out_shape=jax.ShapeDtypeStruct((slots, width), bf),
        in_specs=[SMEM] + [VMEM] * 5,
        out_specs=VMEM,
        compiler_params=PARAMS,
    )(place, all_hidden, w_down, moved[0], moved[1], swapped)
    back = lax.all_to_all(
        piece.reshape(dp_count, CAP, width), "dp", split_axis=0, concat_axis=0, tiled=True
    )
    spread = pl.pallas_call(
        spread_kernel,
        out_shape=jax.ShapeDtypeStruct((tok_rows, width), bf),
        in_specs=[SMEM, VMEM, VMEM],
        out_specs=VMEM,
        compiler_params=PARAMS,
    )(place, routes, back.reshape(slots, width))
    final = lax.all_to_all(
        spread.reshape(owners, tok_rows // owners, width),
        ("g", "j", "k"),
        split_axis=0,
        concat_axis=0,
        tiled=True,
    )
    return pl.pallas_call(
        finish_kernel,
        out_shape=jax.ShapeDtypeStruct((tok_rows // owners, model), bf),
        in_specs=[SMEM, VMEM, VMEM],
        out_specs=VMEM,
        compiler_params=PARAMS,
    )(place, scores, final.reshape(tok_rows, width))


def solution(mesh):
    dp_count, ctx_count = mesh.devices.shape
    split = Mesh(
        mesh.devices.reshape(dp_count, EXP_DP, ctx_count // EXP_DP // CORES, CORES),
        ("dp", "g", "j", "k"),
    )
    everywhere = ("dp", "g", "j", "k")
    in_specs = (
        P("dp", None),
        P("dp", None),
        P("dp", None),
        P(None, everywhere),
        P(None, everywhere),
        P(everywhere, None),
    )
    return jax.shard_map(
        per_device, mesh=split, in_specs=in_specs, out_specs=P(everywhere, None), check_vma=False
    )
```

```python
import functools

import jax
import jax.numpy as jnp
from jax import lax
from jax.experimental import pallas as pl
from jax.experimental.pallas import tpu as pltpu
from jax.sharding import Mesh
from jax.sharding import PartitionSpec as P

EXP_DP = 4
CAP = 4
CORES = 2
LANES = 128
QUARTERS = 4
CHUNK = CAP * QUARTERS
ROUTE_SCALE = 2.5
VMEM_LIMIT = 20 * 1024 * 1024
FAR = 1 << 20
BESIDE = pl.CostEstimate(flops=8 * 10**9, bytes_accessed=16 * 1024 * 1024, transcendentals=0)

VMEM = pl.BlockSpec(memory_space=pltpu.VMEM)
HBM = pl.BlockSpec(memory_space=pltpu.HBM)


def iota(shape, axis):
    return lax.broadcasted_iota(jnp.int32, shape, axis)


def one_hot(mask):
    return jnp.where(mask, 1.0, 0.0).astype(jnp.bfloat16)


def dot(a, b):
    return jnp.dot(a, b, preferred_element_type=jnp.float32)


def slots_of_tokens(routes, group, down):
    tokens = routes.shape[1]
    row, col = iota((tokens, tokens), 0), iota((tokens, tokens), 1)
    across = jnp.broadcast_to(routes, (tokens, tokens))
    column = jnp.sum(jnp.where(row == col, across, 0), axis=1, keepdims=True)
    same = across == column
    if down:
        rank = jnp.sum((same & (col < row)).astype(jnp.int32), axis=1, keepdims=True)
        own = column
    else:
        rank = jnp.sum((same & (row < col)).astype(jnp.int32), axis=0, keepdims=True)
        own = routes
    slot = (own >> 2) * CAP + rank
    return jnp.where((own & 3) == group, slot, jnp.int32(FAR))


def pick_kernel(routes_ref, tokens_ref, out_ref, row_ref, half_ref, sems):
    rows, width = out_ref.shape
    base = lax.axis_index("k") * (QUARTERS * width)
    copies = [pltpu.make_async_copy(routes_ref, row_ref, sems.at[QUARTERS])]
    for q in range(QUARTERS):
        start = pl.multiple_of(base + q * width, LANES)
        copies.append(
            pltpu.make_async_copy(
                tokens_ref.at[:, pl.ds(start, width)], half_ref.at[q], sems.at[q]
            )
        )
    for copy in copies:
        copy.start()
    copies[0].wait()
    slot = slots_of_tokens(row_ref[...], lax.axis_index("g"), False)
    row = iota((rows, 1), 0)
    wanted = (row >> 4) * CAP + (row & 3)
    total = None
    for q in range(QUARTERS):
        pick = one_hot(jnp.where(((row >> 2) & 3) == q, wanted, -1) == slot)
        copies[1 + q].wait()
        term = dot(pick, half_ref[q])
        total = term if total is None else total + term
    out_ref[...] = total.astype(jnp.bfloat16)


def run(copies):
    for copy in copies:
        copy.start()
    for copy in copies:
        copy.wait()


def away_kernel(down_ref, out_ref, sem):
    half = out_ref.shape[1]
    start = pl.multiple_of((1 - lax.axis_index("k")) * half, LANES)
    run([pltpu.make_async_copy(down_ref.at[:, pl.ds(start, half)], out_ref, sem)])


def blocks_kernel(down_ref, given_ref, *rest):
    blocks, sems = rest[:-1], rest[-1]
    half = given_ref.shape[1]
    copies = []
    for step, block_ref in enumerate(blocks):
        width = block_ref.shape[2]
        start = jnp.minimum(lax.rem(lax.axis_index("j") + step, 3) * width, half - width)
        starts = (lax.axis_index("k") * half + start, start)
        for which, (ref, at) in enumerate(zip((down_ref, given_ref), starts)):
            copies.append(
                pltpu.make_async_copy(
                    ref.at[:, pl.ds(pl.multiple_of(at, LANES), width)],
                    block_ref.at[which],
                    sems.at[CORES * step + which],
                )
            )
    run(copies)


def join_kernel(own, gate_ref, up_ref, out_ref, sems):
    half, units = out_ref.shape[0], gate_ref.shape[1]
    me = lax.axis_index("k")
    start = pl.multiple_of((me if own else 1 - me) * half, LANES)
    run(
        [
            pltpu.make_async_copy(
                w_ref.at[pl.ds(start, half)], out_ref.at[:, pl.ds(at * units, units)], sems.at[at]
            )
            for at, w_ref in enumerate((gate_ref, up_ref))
        ]
    )


def unpack(slots, rows, q):
    slot, row = iota((slots, rows), 0), iota((slots, rows), 1)
    return one_hot(row == (slot >> 2) * CHUNK + q * CAP + (slot & 3))


def project(chunks_ref, weights_ref, slots):
    rows, width = chunks_ref.shape
    chunks = chunks_ref[...]
    total = None
    for q in range(QUARTERS):
        part = dot(unpack(slots, rows, q), chunks).astype(jnp.bfloat16)
        term = dot(part, weights_ref[q * width : (q + 1) * width, :])
        total = term if total is None else total + term
    return total


def own_kernel(chunks_ref, weights_ref, out_ref):
    out_ref[...] = project(chunks_ref, weights_ref, out_ref.shape[0])


def hidden_kernel(partial_ref, chunks_ref, weights_ref, out_ref):
    slots, units = out_ref.shape
    pre = partial_ref[...] + project(chunks_ref, weights_ref, slots)
    gate, up = pre[:, :units], pre[:, units:]
    out_ref[...] = (gate * jax.nn.sigmoid(gate) * up).astype(jnp.bfloat16)


def down_kernel(hidden_ref, kept_ref, next_ref, last_ref, out_ref):
    slots = hidden_ref.shape[1]
    rows, width = out_ref.shape
    columns = next_ref.shape[2]
    third, core = lax.axis_index("j"), lax.axis_index("k")
    total = None
    for step, weights in enumerate((kept_ref, next_ref, last_ref)):
        source = lax.rem(third + 3 - step, 3)
        for which in range(CORES):
            who = core if which == 0 else 1 - core
            term = dot(hidden_ref[CORES * source + who], weights[which])
            total = term if total is None else total + term
    piece = total.astype(jnp.bfloat16)
    out = None
    row, slot = iota((rows, slots), 0), iota((rows, slots), 1)
    hit = slot == (row >> 4) * CAP + (row & 3)
    for q in range(QUARTERS):
        block = piece[:, q * width : min(columns, (q + 1) * width)]
        if block.shape[1] < width:
            block = jnp.concatenate(
                [block, jnp.zeros((slots, width - block.shape[1]), block.dtype)], axis=1
            )
        term = dot(one_hot(hit & (((row >> 2) & 3) == q)), block)
        out = term if out is None else out + term
    out_ref[...] = out.astype(jnp.bfloat16)


def spread_kernel(routes_ref, back_ref, out_ref):
    rows, width = back_ref.shape
    tokens, columns = out_ref.shape
    slot = slots_of_tokens(routes_ref[...], lax.axis_index("g"), True)
    first = (slot >> 2) * CHUNK + (slot & 3)
    row = iota((tokens, rows), 1)
    back = back_ref[...]
    for q in range(QUARTERS):
        stop = min(columns, (q + 1) * width)
        block = dot(one_hot(row == first + q * CAP), back[:, : stop - q * width])
        out_ref[:, q * width : stop] = block.astype(jnp.bfloat16)


def finish_kernel(scores_ref, parts_ref, out_ref):
    rows, model = out_ref.shape
    width = parts_ref.shape[1]
    tokens = scores_ref.shape[1]
    sig = jax.nn.sigmoid(scores_ref[...])
    gates = ROUTE_SCALE * sig[:1] / jnp.sum(sig, axis=0, keepdims=True)
    owner = (lax.axis_index("g") * lax.axis_size("j") + lax.axis_index("j")) * CORES
    owner += lax.axis_index("k")
    mine = iota((rows, tokens), 1) == owner * rows + iota((rows, tokens), 0)
    gates = jnp.sum(jnp.where(mine, gates, 0.0), axis=1, keepdims=True)
    parts = parts_ref[...].astype(jnp.float32)
    per_group = parts.shape[0] // EXP_DP
    total = parts[:per_group]
    for group in range(1, EXP_DP):
        total = total + parts[group * per_group : (group + 1) * per_group]
    half = model // CORES
    for part in range(per_group // rows):
        third, core = part // CORES, part % CORES
        base = min(third * width, half - width)
        skip = third * width - base
        block = total[part * rows : (part + 1) * rows, skip:] * gates
        base += core * half
        out_ref[:, base + skip : base + width] = block.astype(jnp.bfloat16)


def call(kernel, shapes, in_specs, args, limit=VMEM_LIMIT, **more):
    single = not isinstance(shapes, list)
    return pl.pallas_call(
        kernel,
        out_shape=shapes,
        in_specs=in_specs,
        out_specs=VMEM if single else [VMEM] * len(shapes),
        compiler_params=pltpu.CompilerParams(vmem_limit_bytes=limit),
        **more,
    )(*args)


def in_hbm(x):
    return pltpu.with_memory_space_constraint(x, pltpu.HBM)


def exchange(x):
    return lax.ppermute(x, "k", [(0, 1), (1, 0)])


def over_dp(x):
    return lax.all_to_all(x, "dp", split_axis=0, concat_axis=0, tiled=True)


def per_device(tokens, scores, routes, w_gate, w_up, w_down):
    dp_count = lax.axis_size("dp")
    tok_rows, model = tokens.shape
    units = w_down.shape[0]
    thirds = lax.axis_size("j")
    owners = EXP_DP * thirds * CORES
    slots = dp_count * CAP
    half = model // CORES
    width = -(-model // (thirds * CORES * LANES)) * LANES
    quarter = -(-width // (QUARTERS * LANES)) * LANES
    bf, f32 = jnp.bfloat16, jnp.float32
    routes_row, scores_row = routes.reshape(1, tok_rows), scores.T

    def array(shape, dtype=bf):
        return jax.ShapeDtypeStruct(shape, dtype)

    flat = (dp_count * CHUNK, half // QUARTERS)
    outgoing = call(
        pick_kernel,
        array(flat),
        [HBM, HBM],
        (in_hbm(routes_row), in_hbm(tokens)),
        scratch_shapes=[
            pltpu.VMEM((1, tok_rows), jnp.int32),
            pltpu.VMEM((QUARTERS, tok_rows, half // QUARTERS), bf),
            pltpu.SemaphoreType.DMA((QUARTERS + 1,)),
        ],
    )
    arrived = over_dp(outgoing.reshape(dp_count, CHUNK, half // QUARTERS))
    away = call(
        away_kernel,
        array((units, half)),
        [HBM],
        (w_down,),
        scratch_shapes=[pltpu.SemaphoreType.DMA],
    )
    given = exchange(away)
    kept, *sent = call(
        blocks_kernel,
        [pltpu.HBM((CORES, units, width), bf)] + [array((CORES, units, width))] * (thirds - 1),
        [HBM, HBM],
        (w_down, given),
        scratch_shapes=[pltpu.SemaphoreType.DMA((CORES * thirds,))],
    )
    arrived = lax.optimization_barrier((arrived, sent))[0]
    moved = [
        lax.ppermute(block, "j", [(i, (i + step) % thirds) for i in range(thirds)])
        for step, block in enumerate(sent, 1)
    ]
    other = exchange(arrived)

    def joined(own, after):
        gate, up, _ = lax.optimization_barrier((w_gate, w_up, after))
        return call(
            functools.partial(join_kernel, own),
            pltpu.VMEM((half, 2 * units), bf),
            [HBM, HBM],
            (in_hbm(gate), in_hbm(up)),
            scratch_shapes=[pltpu.SemaphoreType.DMA((2,))],
            cost_estimate=None if own else BESIDE,
        )

    other = exchange(arrived)
    partial = call(
        own_kernel,
        array((slots, 2 * units), f32),
        [VMEM] * 2,
        (arrived.reshape(flat), joined(True, sent)),
        cost_estimate=BESIDE,
    )
    hidden = call(
        hidden_kernel,
        array((slots, units)),
        [VMEM] * 3,
        (partial, other.reshape(flat), joined(False, partial)),
    )
    all_hidden = lax.all_gather(hidden, ("j", "k"), axis=0)
    piece = call(
        down_kernel,
        array((dp_count * CHUNK, quarter)),
        [VMEM] * (1 + thirds),
        (all_hidden, kept, *moved),
    )
    back = over_dp(piece.reshape(dp_count, CHUNK, quarter))
    spread = call(
        spread_kernel,
        array((tok_rows, width)),
        [VMEM, VMEM],
        (routes_row, back.reshape(dp_count * CHUNK, quarter)),
    )
    final = lax.all_to_all(
        spread.reshape(owners, tok_rows // owners, width),
        ("g", "j", "k"),
        split_axis=0,
        concat_axis=0,
        tiled=True,
    )
    return call(
        finish_kernel,
        array((tok_rows // owners, model)),
        [VMEM, VMEM],
        (scores_row, final.reshape(tok_rows, width)),
    )


def solution(mesh):
    dp_count, ctx_count = mesh.devices.shape
    split = Mesh(
        mesh.devices.reshape(dp_count, EXP_DP, ctx_count // EXP_DP // CORES, CORES),
        ("dp", "g", "j", "k"),
    )
    everywhere = ("dp", "g", "j", "k")
    in_specs = (
        P("dp", None),
        P("dp", None),
        P("dp", None),
        P(None, everywhere),
        P(None, everywhere),
        P(everywhere, None),
    )
    return jax.shard_map(
        per_device, mesh=split, in_specs=in_specs, out_specs=P(everywhere, None), check_vma=False
    )
```

```python
import functools

import jax
import jax.numpy as jnp
from jax import lax
from jax.experimental import pallas as pl
from jax.experimental.pallas import tpu as pltpu
from jax.sharding import Mesh
from jax.sharding import PartitionSpec as P

EXP_DP = 4
CAP = 4
CORES = 2
LANES = 128
QUARTERS = 4
CHUNK = CAP * QUARTERS
ROUTE_SCALE = 2.5
VMEM_LIMIT = 20 * 1024 * 1024
FAR = 1 << 20
BESIDE = pl.CostEstimate(flops=8 * 10**9, bytes_accessed=16 * 1024 * 1024, transcendentals=0)

VMEM = pl.BlockSpec(memory_space=pltpu.VMEM)
HBM = pl.BlockSpec(memory_space=pltpu.HBM)


def iota(shape, axis):
    return lax.broadcasted_iota(jnp.int32, shape, axis)


def one_hot(mask):
    return jnp.where(mask, 1.0, 0.0).astype(jnp.bfloat16)


def dot(a, b):
    return jnp.dot(a, b, preferred_element_type=jnp.float32)


def slots_of_tokens(routes, group, down):
    tokens = routes.shape[1]
    row, col = iota((tokens, tokens), 0), iota((tokens, tokens), 1)
    across = jnp.broadcast_to(routes, (tokens, tokens))
    column = jnp.sum(jnp.where(row == col, across, 0), axis=1, keepdims=True)
    same = across == column
    if down:
        rank = jnp.sum((same & (col < row)).astype(jnp.int32), axis=1, keepdims=True)
        own = column
    else:
        rank = jnp.sum((same & (row < col)).astype(jnp.int32), axis=0, keepdims=True)
        own = routes
    slot = (own >> 2) * CAP + rank
    return jnp.where((own & 3) == group, slot, jnp.int32(FAR))


def pick_kernel(routes_ref, tokens_ref, out_ref, row_ref, half_ref, sems):
    rows, width = out_ref.shape
    tokens, half = half_ref.shape
    start = pl.multiple_of(lax.axis_index("k") * half, LANES)
    part = tokens // 2
    copies = [pltpu.make_async_copy(routes_ref, row_ref, sems.at[2])]
    for at in range(2):
        span = pl.ds(at * part, part)
        copies.append(
            pltpu.make_async_copy(
                tokens_ref.at[span, pl.ds(start, half)], half_ref.at[span], sems.at[at]
            )
        )
    for copy in copies:
        copy.start()
    copies[0].wait()
    slot = slots_of_tokens(row_ref[...], lax.axis_index("g"), False)
    row = iota((rows, 1), 0)
    wanted = (row >> 4) * CAP + (row & 3)
    picks = [
        one_hot(jnp.where(((row >> 2) & 3) == q, wanted, -1) == slot) for q in range(QUARTERS)
    ]
    for copy in copies[1:]:
        copy.wait()
    total = None
    for q in range(QUARTERS):
        term = dot(picks[q], half_ref[:, q * width : (q + 1) * width])
        total = term if total is None else total + term
    out_ref[...] = total.astype(jnp.bfloat16)


def run(copies):
    for copy in copies:
        copy.start()
    for copy in copies:
        copy.wait()


def blocks_kernel(down_ref, *rest):
    blocks, sems = rest[:-1], rest[-1]
    model = down_ref.shape[1]
    copies = []
    for at, block_ref in enumerate(blocks):
        width = block_ref.shape[1]
        to = lax.rem(lax.axis_index("j") + at + 1, 3)
        start = pl.multiple_of(jnp.minimum(to * width, model - width), LANES)
        copies.append(
            pltpu.make_async_copy(down_ref.at[:, pl.ds(start, width)], block_ref, sems.at[at])
        )
    run(copies)


def join_kernel(own, gate_ref, up_ref, out_ref, sems):
    half, units = out_ref.shape[0], gate_ref.shape[1]
    me = lax.axis_index("k")
    start = pl.multiple_of((me if own else 1 - me) * half, LANES)
    run(
        [
            pltpu.make_async_copy(
                w_ref.at[pl.ds(start, half)], out_ref.at[:, pl.ds(at * units, units)], sems.at[at]
            )
            for at, w_ref in enumerate((gate_ref, up_ref))
        ]
    )


def unpack(slots, rows, q):
    slot, row = iota((slots, rows), 0), iota((slots, rows), 1)
    return one_hot(row == (slot >> 2) * CHUNK + q * CAP + (slot & 3))


def project(chunks_ref, weights_ref, slots):
    rows, width = chunks_ref.shape
    chunks = chunks_ref[...]
    total = None
    for q in range(QUARTERS):
        part = dot(unpack(slots, rows, q), chunks).astype(jnp.bfloat16)
        term = dot(part, weights_ref[q * width : (q + 1) * width, :])
        total = term if total is None else total + term
    return total


def own_kernel(chunks_ref, weights_ref, out_ref):
    out_ref[...] = project(chunks_ref, weights_ref, out_ref.shape[0])


def hidden_kernel(partial_ref, chunks_ref, weights_ref, out_ref):
    slots, units = out_ref.shape
    pre = partial_ref[...] + project(chunks_ref, weights_ref, slots)
    gate, up = pre[:, :units], pre[:, units:]
    out_ref[...] = (gate * jax.nn.sigmoid(gate) * up).astype(jnp.bfloat16)


def down_kernel(hidden_ref, next_ref, last_ref, kept_ref, mine_ref, sent_ref):
    width = mine_ref.shape[1]
    third, core = lax.axis_index("j"), lax.axis_index("k")
    for out_ref, who in ((sent_ref, 1 - core), (mine_ref, core)):
        columns = pl.ds(pl.multiple_of(who * width, LANES), width)
        total = None
        for step, weights_ref in ((0, kept_ref), (1, next_ref), (2, last_ref)):
            source = lax.rem(third + 3 - step, 3)
            term = dot(hidden_ref[source], weights_ref[:, columns])
            total = term if total is None else total + term
        out_ref[...] = total.astype(out_ref.dtype)


def pack_kernel(mine_ref, sent_ref, out_ref):
    slots, columns = mine_ref.shape
    rows, width = out_ref.shape
    piece = (mine_ref[...] + sent_ref[1 - lax.axis_index("k")].astype(jnp.float32)).astype(
        jnp.bfloat16
    )
    out = None
    row, slot = iota((rows, slots), 0), iota((rows, slots), 1)
    hit = slot == (row >> 4) * CAP + (row & 3)
    for q in range(QUARTERS):
        block = piece[:, q * width : min(columns, (q + 1) * width)]
        if block.shape[1] < width:
            block = jnp.concatenate(
                [block, jnp.zeros((slots, width - block.shape[1]), block.dtype)], axis=1
            )
        term = dot(one_hot(hit & (((row >> 2) & 3) == q)), block)
        out = term if out is None else out + term
    out_ref[...] = out.astype(jnp.bfloat16)


def spread_kernel(routes_ref, back_ref, out_ref):
    rows, width = back_ref.shape
    tokens, columns = out_ref.shape
    slot = slots_of_tokens(routes_ref[...], lax.axis_index("g"), True)
    first = (slot >> 2) * CHUNK + (slot & 3)
    row = iota((tokens, rows), 1)
    back = back_ref[...]
    for q in range(QUARTERS):
        stop = min(columns, (q + 1) * width)
        block = dot(one_hot(row == first + q * CAP), back[:, : stop - q * width])
        out_ref[:, q * width : stop] = block.astype(jnp.bfloat16)


def finish_kernel(scores_ref, parts_ref, out_ref):
    rows, model = out_ref.shape
    width = parts_ref.shape[1]
    tokens = scores_ref.shape[1]
    sig = jax.nn.sigmoid(scores_ref[...])
    gates = ROUTE_SCALE * sig[:1] / jnp.sum(sig, axis=0, keepdims=True)
    owner = (lax.axis_index("g") * lax.axis_size("j") + lax.axis_index("j")) * CORES
    owner += lax.axis_index("k")
    mine = iota((rows, tokens), 1) == owner * rows + iota((rows, tokens), 0)
    gates = jnp.sum(jnp.where(mine, gates, 0.0), axis=1, keepdims=True)
    parts = parts_ref[...].astype(jnp.float32)
    per_group = parts.shape[0] // EXP_DP
    total = parts[:per_group]
    for group in range(1, EXP_DP):
        total = total + parts[group * per_group : (group + 1) * per_group]
    for part in range(per_group // rows):
        third, core = part // CORES, part % CORES
        base = min(third * CORES * width, model - CORES * width) + core * width
        skip = max(0, part * width - base) if core == 0 else 0
        block = total[part * rows : (part + 1) * rows, skip:] * gates
        out_ref[:, base + skip : base + width] = block.astype(jnp.bfloat16)


def call(kernel, shapes, in_specs, args, limit=VMEM_LIMIT, **more):
    single = not isinstance(shapes, list)
    return pl.pallas_call(
        kernel,
        out_shape=shapes,
        in_specs=in_specs,
        out_specs=VMEM if single else [VMEM] * len(shapes),
        compiler_params=pltpu.CompilerParams(vmem_limit_bytes=limit),
        **more,
    )(*args)


def in_hbm(x):
    return pltpu.with_memory_space_constraint(x, pltpu.HBM)


def exchange(x):
    return lax.ppermute(x, "k", [(0, 1), (1, 0)])


def over_dp(x):
    return lax.all_to_all(x, "dp", split_axis=0, concat_axis=0, tiled=True)


def per_device(tokens, scores, routes, w_gate, w_up, w_down):
    dp_count = lax.axis_size("dp")
    tok_rows, model = tokens.shape
    units = w_down.shape[0]
    thirds = lax.axis_size("j")
    owners = EXP_DP * thirds * CORES
    slots = dp_count * CAP
    half = model // CORES
    width = -(-model // (thirds * CORES * LANES)) * LANES
    quarter = -(-width // (QUARTERS * LANES)) * LANES
    bf, f32 = jnp.bfloat16, jnp.float32
    routes_row, scores_row = routes.reshape(1, tok_rows), scores.T

    def array(shape, dtype=bf):
        return jax.ShapeDtypeStruct(shape, dtype)

    flat = (dp_count * CHUNK, half // QUARTERS)
    outgoing = call(
        pick_kernel,
        array(flat),
        [HBM, HBM],
        (in_hbm(routes_row), in_hbm(tokens)),
        scratch_shapes=[
            pltpu.VMEM((1, tok_rows), jnp.int32),
            pltpu.VMEM((tok_rows, half), bf),
            pltpu.SemaphoreType.DMA((3,)),
        ],
    )
    arrived = over_dp(outgoing.reshape(dp_count, CHUNK, half // QUARTERS))
    *sent, kept = call(
        blocks_kernel,
        [array((units, CORES * width))] * thirds,
        [HBM],
        (w_down,),
        scratch_shapes=[pltpu.SemaphoreType.DMA((thirds,))],
    )
    arrived = lax.optimization_barrier((arrived, sent))[0]
    moved = [
        lax.ppermute(block, "j", [(i, (i + step) % thirds) for i in range(thirds)])
        for step, block in enumerate(sent, 1)
    ]
    other = exchange(arrived)

    def joined(own, after):
        gate, up, _ = lax.optimization_barrier((w_gate, w_up, after))
        return call(
            functools.partial(join_kernel, own),
            pltpu.VMEM((half, 2 * units), bf),
            [HBM, HBM],
            (in_hbm(gate), in_hbm(up)),
            scratch_shapes=[pltpu.SemaphoreType.DMA((2,))],
            cost_estimate=None if own else BESIDE,
        )

    other = exchange(arrived)
    partial = call(
        own_kernel,
        array((slots, 2 * units), f32),
        [VMEM] * 2,
        (arrived.reshape(flat), joined(True, sent)),
        cost_estimate=BESIDE,
    )
    hidden = call(
        hidden_kernel,
        array((slots, units)),
        [VMEM] * 3,
        (partial, other.reshape(flat), joined(False, partial)),
    )
    all_hidden = lax.all_gather(hidden, "j", axis=0)
    mine, others = call(
        down_kernel,
        [array((slots, width), f32), array((slots, width))],
        [VMEM] * (1 + thirds),
        (all_hidden, *moved, kept),
    )
    piece = call(
        pack_kernel,
        array((dp_count * CHUNK, quarter)),
        [VMEM] * 2,
        (mine, lax.all_gather(others, "k", axis=0)),
    )
    back = over_dp(piece.reshape(dp_count, CHUNK, quarter))
    spread = call(
        spread_kernel,
        array((tok_rows, width)),
        [VMEM, VMEM],
        (routes_row, back.reshape(dp_count * CHUNK, quarter)),
    )
    final = lax.all_to_all(
        spread.reshape(owners, tok_rows // owners, width),
        ("g", "j", "k"),
        split_axis=0,
        concat_axis=0,
        tiled=True,
    )
    return call(
        finish_kernel,
        array((tok_rows // owners, model)),
        [VMEM, VMEM],
        (scores_row, final.reshape(tok_rows, width)),
    )


def solution(mesh):
    dp_count, ctx_count = mesh.devices.shape
    split = Mesh(
        mesh.devices.reshape(dp_count, EXP_DP, ctx_count // EXP_DP // CORES, CORES),
        ("dp", "g", "j", "k"),
    )
    everywhere = ("dp", "g", "j", "k")
    in_specs = (
        P("dp", None),
        P("dp", None),
        P("dp", None),
        P(None, everywhere),
        P(None, everywhere),
        P(everywhere, None),
    )
    return jax.shard_map(
        per_device, mesh=split, in_specs=in_specs, out_specs=P(everywhere, None), check_vma=False
    )
```

```python
import functools

import jax
import jax.numpy as jnp
from jax import lax
from jax.experimental import pallas as pl
from jax.experimental.pallas import tpu as pltpu
from jax.sharding import Mesh
from jax.sharding import PartitionSpec as P

EXP_DP = 4
CAP = 4
CORES = 2
LANES = 128
QUARTERS = 4
CHUNK = CAP * QUARTERS
ROUTE_SCALE = 2.5
VMEM_LIMIT = 20 * 1024 * 1024
FAR = 1 << 20
BESIDE = pl.CostEstimate(flops=8 * 10**9, bytes_accessed=16 * 1024 * 1024, transcendentals=0)

VMEM = pl.BlockSpec(memory_space=pltpu.VMEM)
HBM = pl.BlockSpec(memory_space=pltpu.HBM)


def iota(shape, axis):
    return lax.broadcasted_iota(jnp.int32, shape, axis)


def one_hot(mask):
    return jnp.where(mask, 1.0, 0.0).astype(jnp.bfloat16)


def dot(a, b):
    return jnp.dot(a, b, preferred_element_type=jnp.float32)


def slots_of_tokens(routes, group, down):
    tokens = routes.shape[1]
    row, col = iota((tokens, tokens), 0), iota((tokens, tokens), 1)
    across = jnp.broadcast_to(routes, (tokens, tokens))
    column = jnp.sum(jnp.where(row == col, across, 0), axis=1, keepdims=True)
    same = across == column
    if down:
        rank = jnp.sum((same & (col < row)).astype(jnp.int32), axis=1, keepdims=True)
        own = column
    else:
        rank = jnp.sum((same & (row < col)).astype(jnp.int32), axis=0, keepdims=True)
        own = routes
    slot = (own >> 2) * CAP + rank
    return jnp.where((own & 3) == group, slot, jnp.int32(FAR))


def pick_kernel(routes_ref, tokens_ref, out_ref, row_ref, half_ref, sems):
    rows, width = out_ref.shape
    tokens, half = half_ref.shape
    start = pl.multiple_of(lax.axis_index("k") * half, LANES)
    part = tokens // 2
    copies = [pltpu.make_async_copy(routes_ref, row_ref, sems.at[2])]
    for at in range(2):
        span = pl.ds(at * part, part)
        copies.append(
            pltpu.make_async_copy(
                tokens_ref.at[span, pl.ds(start, half)], half_ref.at[span], sems.at[at]
            )
        )
    for copy in copies:
        copy.start()
    copies[0].wait()
    slot = slots_of_tokens(row_ref[...], lax.axis_index("g"), False)
    row = iota((rows, 1), 0)
    wanted = (row >> 4) * CAP + (row & 3)
    picks = [
        one_hot(jnp.where(((row >> 2) & 3) == q, wanted, -1) == slot) for q in range(QUARTERS)
    ]
    for copy in copies[1:]:
        copy.wait()
    total = None
    for q in range(QUARTERS):
        term = dot(picks[q], half_ref[:, q * width : (q + 1) * width])
        total = term if total is None else total + term
    out_ref[...] = total.astype(jnp.bfloat16)


def run(copies):
    for copy in copies:
        copy.start()
    for copy in copies:
        copy.wait()


def blocks_kernel(down_ref, *rest):
    blocks, sems = rest[:-1], rest[-1]
    model = down_ref.shape[1]
    copies = []
    for at, block_ref in enumerate(blocks):
        width = block_ref.shape[1]
        to = lax.rem(lax.axis_index("j") + at + 1, 3)
        start = pl.multiple_of(jnp.minimum(to * width, model - width), LANES)
        copies.append(
            pltpu.make_async_copy(down_ref.at[:, pl.ds(start, width)], block_ref, sems.at[at])
        )
    run(copies)


def join_kernel(own, gate_ref, up_ref, out_ref, sems):
    half, units = out_ref.shape[0], gate_ref.shape[1]
    me = lax.axis_index("k")
    start = pl.multiple_of((me if own else 1 - me) * half, LANES)
    run(
        [
            pltpu.make_async_copy(
                w_ref.at[pl.ds(start, half)], out_ref.at[:, pl.ds(at * units, units)], sems.at[at]
            )
            for at, w_ref in enumerate((gate_ref, up_ref))
        ]
    )


def unpack(slots, rows, q):
    slot, row = iota((slots, rows), 0), iota((slots, rows), 1)
    return one_hot(row == (slot >> 2) * CHUNK + q * CAP + (slot & 3))


def project(chunks_ref, weights_ref, slots):
    rows, width = chunks_ref.shape
    chunks = chunks_ref[...]
    total = None
    for q in range(QUARTERS):
        part = dot(unpack(slots, rows, q), chunks).astype(jnp.bfloat16)
        term = dot(part, weights_ref[q * width : (q + 1) * width, :])
        total = term if total is None else total + term
    return total


def own_kernel(chunks_ref, weights_ref, out_ref):
    out_ref[...] = project(chunks_ref, weights_ref, out_ref.shape[0])


def hidden_kernel(partial_ref, chunks_ref, weights_ref, out_ref):
    slots, units = out_ref.shape
    pre = partial_ref[...] + project(chunks_ref, weights_ref, slots)
    gate, up = pre[:, :units], pre[:, units:]
    out_ref[...] = (gate * jax.nn.sigmoid(gate) * up).astype(jnp.bfloat16)


def down_kernel(hidden_ref, next_ref, last_ref, kept_ref, mine_ref, sent_ref):
    width = mine_ref.shape[1]
    third, core = lax.axis_index("j"), lax.axis_index("k")
    for out_ref, who in ((sent_ref, 1 - core), (mine_ref, core)):
        columns = pl.ds(pl.multiple_of(who * width, LANES), width)
        total = None
        for step, weights_ref in ((0, kept_ref), (1, next_ref), (2, last_ref)):
            source = lax.rem(third + 3 - step, 3)
            term = dot(hidden_ref[source], weights_ref[:, columns])
            total = term if total is None else total + term
        out_ref[...] = total.astype(out_ref.dtype)


def pack_kernel(mine_ref, sent_ref, out_ref):
    slots, columns = mine_ref.shape
    rows, width = out_ref.shape
    piece = (mine_ref[...] + sent_ref[1 - lax.axis_index("k")].astype(jnp.float32)).astype(
        jnp.bfloat16
    )
    out = None
    row, slot = iota((rows, slots), 0), iota((rows, slots), 1)
    hit = slot == (row >> 4) * CAP + (row & 3)
    for q in range(QUARTERS):
        block = piece[:, q * width : min(columns, (q + 1) * width)]
        if block.shape[1] < width:
            block = jnp.concatenate(
                [block, jnp.zeros((slots, width - block.shape[1]), block.dtype)], axis=1
            )
        term = dot(one_hot(hit & (((row >> 2) & 3) == q)), block)
        out = term if out is None else out + term
    out_ref[...] = out.astype(jnp.bfloat16)


def ahead_kernel(routes_ref, scores_ref, first_ref, gates_ref):
    slot = slots_of_tokens(routes_ref[...], lax.axis_index("g"), True)
    first_ref[...] = (slot >> 2) * CHUNK + (slot & 3)
    rows, tokens = gates_ref.shape[0], scores_ref.shape[1]
    sig = jax.nn.sigmoid(scores_ref[...])
    gates = ROUTE_SCALE * sig[:1] / jnp.sum(sig, axis=0, keepdims=True)
    owner = (lax.axis_index("g") * lax.axis_size("j") + lax.axis_index("j")) * CORES
    owner += lax.axis_index("k")
    mine = iota((rows, tokens), 1) == owner * rows + iota((rows, tokens), 0)
    gates_ref[...] = jnp.sum(jnp.where(mine, gates, 0.0), axis=1, keepdims=True)


def spread_kernel(first_ref, back_ref, out_ref):
    rows, width = back_ref.shape
    tokens, columns = out_ref.shape
    first = first_ref[...]
    row = iota((tokens, rows), 1)
    back = back_ref[...]
    for q in range(QUARTERS):
        stop = min(columns, (q + 1) * width)
        block = dot(one_hot(row == first + q * CAP), back[:, : stop - q * width])
        out_ref[:, q * width : stop] = block.astype(jnp.bfloat16)


def finish_kernel(gates_ref, parts_ref, out_ref):
    rows, model = out_ref.shape
    width = parts_ref.shape[1]
    gates = gates_ref[...]
    parts = parts_ref[...].astype(jnp.float32)
    per_group = parts.shape[0] // EXP_DP
    total = parts[:per_group]
    for group in range(1, EXP_DP):
        total = total + parts[group * per_group : (group + 1) * per_group]
    for part in range(per_group // rows):
        third, core = part // CORES, part % CORES
        base = min(third * CORES * width, model - CORES * width) + core * width
        skip = max(0, part * width - base) if core == 0 else 0
        block = total[part * rows : (part + 1) * rows, skip:] * gates
        out_ref[:, base + skip : base + width] = block.astype(jnp.bfloat16)


def call(kernel, shapes, in_specs, args, limit=VMEM_LIMIT, **more):
    single = not isinstance(shapes, list)
    return pl.pallas_call(
        kernel,
        out_shape=shapes,
        in_specs=in_specs,
        out_specs=VMEM if single else [VMEM] * len(shapes),
        compiler_params=pltpu.CompilerParams(vmem_limit_bytes=limit),
        **more,
    )(*args)


def in_hbm(x):
    return pltpu.with_memory_space_constraint(x, pltpu.HBM)


def exchange(x):
    return lax.ppermute(x, "k", [(0, 1), (1, 0)])


def over_dp(x):
    return lax.all_to_all(x, "dp", split_axis=0, concat_axis=0, tiled=True)


def per_device(tokens, scores, routes, w_gate, w_up, w_down):
    dp_count = lax.axis_size("dp")
    tok_rows, model = tokens.shape
    units = w_down.shape[0]
    thirds = lax.axis_size("j")
    owners = EXP_DP * thirds * CORES
    slots = dp_count * CAP
    half = model // CORES
    width = -(-model // (thirds * CORES * LANES)) * LANES
    quarter = -(-width // (QUARTERS * LANES)) * LANES
    bf, f32 = jnp.bfloat16, jnp.float32
    routes_row, scores_row = routes.reshape(1, tok_rows), scores.T

    def array(shape, dtype=bf):
        return jax.ShapeDtypeStruct(shape, dtype)

    flat = (dp_count * CHUNK, half // QUARTERS)
    outgoing = call(
        pick_kernel,
        array(flat),
        [HBM, HBM],
        (in_hbm(routes_row), in_hbm(tokens)),
        scratch_shapes=[
            pltpu.VMEM((1, tok_rows), jnp.int32),
            pltpu.VMEM((tok_rows, half), bf),
            pltpu.SemaphoreType.DMA((3,)),
        ],
    )
    arrived = over_dp(outgoing.reshape(dp_count, CHUNK, half // QUARTERS))
    *sent, kept = call(
        blocks_kernel,
        [array((units, CORES * width))] * thirds,
        [HBM],
        (w_down,),
        scratch_shapes=[pltpu.SemaphoreType.DMA((thirds,))],
    )
    first, gates = call(
        ahead_kernel,
        [array((tok_rows, 1), jnp.int32), array((tok_rows // owners, 1), f32)],
        [VMEM] * 2,
        lax.optimization_barrier((routes_row, scores_row, sent))[:2],
    )
    arrived = lax.optimization_barrier((arrived, sent, first, gates))[0]
    moved = [
        lax.ppermute(block, "j", [(i, (i + step) % thirds) for i in range(thirds)])
        for step, block in enumerate(sent, 1)
    ]
    other = exchange(arrived)

    def joined(own, after):
        gate, up, _ = lax.optimization_barrier((w_gate, w_up, after))
        return call(
            functools.partial(join_kernel, own),
            pltpu.VMEM((half, 2 * units), bf),
            [HBM, HBM],
            (in_hbm(gate), in_hbm(up)),
            scratch_shapes=[pltpu.SemaphoreType.DMA((2,))],
            cost_estimate=None if own else BESIDE,
        )

    other = exchange(arrived)
    partial = call(
        own_kernel,
        array((slots, 2 * units), f32),
        [VMEM] * 2,
        (arrived.reshape(flat), joined(True, sent)),
        cost_estimate=BESIDE,
    )
    hidden = call(
        hidden_kernel,
        array((slots, units)),
        [VMEM] * 3,
        (partial, other.reshape(flat), joined(False, partial)),
    )
    all_hidden = lax.all_gather(hidden, "j", axis=0)
    mine, others = call(
        down_kernel,
        [array((slots, width), f32), array((slots, width))],
        [VMEM] * (1 + thirds),
        (all_hidden, *moved, kept),
    )
    piece = call(
        pack_kernel,
        array((dp_count * CHUNK, quarter)),
        [VMEM] * 2,
        (mine, lax.all_gather(others, "k", axis=0)),
    )
    back = over_dp(piece.reshape(dp_count, CHUNK, quarter))
    spread = call(
        spread_kernel,
        array((tok_rows, width)),
        [VMEM, VMEM],
        (first, back.reshape(dp_count * CHUNK, quarter)),
    )
    final = lax.all_to_all(
        spread.reshape(owners, tok_rows // owners, width),
        ("g", "j", "k"),
        split_axis=0,
        concat_axis=0,
        tiled=True,
    )
    return call(
        finish_kernel,
        array((tok_rows // owners, model)),
        [VMEM, VMEM],
        (gates, final.reshape(tok_rows, width)),
    )


def solution(mesh):
    dp_count, ctx_count = mesh.devices.shape
    split = Mesh(
        mesh.devices.reshape(dp_count, EXP_DP, ctx_count // EXP_DP // CORES, CORES),
        ("dp", "g", "j", "k"),
    )
    everywhere = ("dp", "g", "j", "k")
    in_specs = (
        P("dp", None),
        P("dp", None),
        P("dp", None),
        P(None, everywhere),
        P(None, everywhere),
        P(everywhere, None),
    )
    return jax.shard_map(
        per_device, mesh=split, in_specs=in_specs, out_specs=P(everywhere, None), check_vma=False
    )
```

```python
import jax
import jax.numpy as jnp
from jax import lax
from jax.experimental import pallas as pl
from jax.experimental.pallas import tpu as pltpu
from jax.sharding import Mesh
from jax.sharding import PartitionSpec as P

EXP_DP = 4
CAP = 4
CORES = 2
LANES = 128
QUARTERS = 4
CHUNK = CAP * QUARTERS
ROUTE_SCALE = 2.5
VMEM_LIMIT = 20 * 1024 * 1024
FAR = 1 << 20
BESIDE = pl.CostEstimate(flops=8 * 10**9, bytes_accessed=16 * 1024 * 1024, transcendentals=0)

VMEM = pl.BlockSpec(memory_space=pltpu.VMEM)
HBM = pl.BlockSpec(memory_space=pltpu.HBM)


def iota(shape, axis):
    return lax.broadcasted_iota(jnp.int32, shape, axis)


def one_hot(mask):
    return jnp.where(mask, 1.0, 0.0).astype(jnp.bfloat16)


def dot(a, b):
    return jnp.dot(a, b, preferred_element_type=jnp.float32)


def slots_of_tokens(routes, group, down):
    tokens = routes.shape[1]
    row, col = iota((tokens, tokens), 0), iota((tokens, tokens), 1)
    across = jnp.broadcast_to(routes, (tokens, tokens))
    column = jnp.sum(jnp.where(row == col, across, 0), axis=1, keepdims=True)
    same = across == column
    if down:
        rank = jnp.sum((same & (col < row)).astype(jnp.int32), axis=1, keepdims=True)
        own = column
    else:
        rank = jnp.sum((same & (row < col)).astype(jnp.int32), axis=0, keepdims=True)
        own = routes
    slot = (own >> 2) * CAP + rank
    return jnp.where((own & 3) == group, slot, jnp.int32(FAR))


def pick_kernel(routes_ref, tokens_ref, out_ref, row_ref, half_ref, sems):
    rows, width = out_ref.shape
    tokens, half = half_ref.shape
    start = pl.multiple_of(lax.axis_index("k") * half, LANES)
    part = tokens // 2
    copies = [pltpu.make_async_copy(routes_ref, row_ref, sems.at[2])]
    for at in range(2):
        span = pl.ds(at * part, part)
        copies.append(
            pltpu.make_async_copy(
                tokens_ref.at[span, pl.ds(start, half)], half_ref.at[span], sems.at[at]
            )
        )
    for copy in copies:
        copy.start()
    copies[0].wait()
    slot = slots_of_tokens(row_ref[...], lax.axis_index("g"), False)
    row = iota((rows, 1), 0)
    wanted = (row >> 4) * CAP + (row & 3)
    picks = [
        one_hot(jnp.where(((row >> 2) & 3) == q, wanted, -1) == slot) for q in range(QUARTERS)
    ]
    for copy in copies[1:]:
        copy.wait()
    total = None
    for q in range(QUARTERS):
        term = dot(picks[q], half_ref[:, q * width : (q + 1) * width])
        total = term if total is None else total + term
    out_ref[...] = total.astype(jnp.bfloat16)


def run(copies):
    for copy in copies:
        copy.start()
    for copy in copies:
        copy.wait()


def blocks_kernel(down_ref, *rest):
    blocks, sems = rest[:-1], rest[-1]
    model = down_ref.shape[1]
    copies = []
    for at, block_ref in enumerate(blocks):
        width = block_ref.shape[1]
        to = lax.rem(lax.axis_index("j") + at + 1, 3)
        start = pl.multiple_of(jnp.minimum(to * width, model - width), LANES)
        copies.append(
            pltpu.make_async_copy(down_ref.at[:, pl.ds(start, width)], block_ref, sems.at[at])
        )
    run(copies)


def stage_kernel(from_ref, out_ref, sem):
    run([pltpu.make_async_copy(from_ref, out_ref, sem)])


def unpack(slots, rows, q):
    slot, row = iota((slots, rows), 0), iota((slots, rows), 1)
    return one_hot(row == (slot >> 2) * CHUNK + q * CAP + (slot & 3))


def project(core, chunks_ref, gate_ref, up_ref, slots):
    rows, width = chunks_ref.shape
    chunks = chunks_ref[...]
    totals = [None, None]
    for q in range(QUARTERS):
        part = dot(unpack(slots, rows, q), chunks).astype(jnp.bfloat16)
        columns = pl.ds(pl.multiple_of((core * QUARTERS + q) * width, LANES), width)
        for at, weights_ref in enumerate((gate_ref, up_ref)):
            term = dot(part, weights_ref[columns, :])
            totals[at] = term if totals[at] is None else totals[at] + term
    return totals


def own_kernel(chunks_ref, gate_ref, up_ref, pre_gate_ref, pre_up_ref):
    pre_gate_ref[...], pre_up_ref[...] = project(
        lax.axis_index("k"), chunks_ref, gate_ref, up_ref, pre_up_ref.shape[0]
    )


def hidden_kernel(pre_gate_ref, pre_up_ref, chunks_ref, gate_ref, up_ref, out_ref):
    core = 1 - lax.axis_index("k")
    gate, up = project(core, chunks_ref, gate_ref, up_ref, out_ref.shape[0])
    gate += pre_gate_ref[...]
    up += pre_up_ref[...]
    out_ref[...] = (gate * jax.nn.sigmoid(gate) * up).astype(jnp.bfloat16)


def down_kernel(hidden_ref, next_ref, last_ref, kept_ref, mine_ref, sent_ref):
    width = mine_ref.shape[1]
    third, core = lax.axis_index("j"), lax.axis_index("k")
    for out_ref, who in ((sent_ref, 1 - core), (mine_ref, core)):
        columns = pl.ds(pl.multiple_of(who * width, LANES), width)
        total = None
        for step, weights_ref in ((0, kept_ref), (1, next_ref), (2, last_ref)):
            source = lax.rem(third + 3 - step, 3)
            term = dot(hidden_ref[source], weights_ref[:, columns])
            total = term if total is None else total + term
        out_ref[...] = total.astype(out_ref.dtype)


def pack_kernel(mine_ref, sent_ref, out_ref):
    slots, columns = mine_ref.shape
    rows, width = out_ref.shape
    piece = (mine_ref[...] + sent_ref[1 - lax.axis_index("k")].astype(jnp.float32)).astype(
        jnp.bfloat16
    )
    out = None
    row, slot = iota((rows, slots), 0), iota((rows, slots), 1)
    hit = slot == (row >> 4) * CAP + (row & 3)
    for q in range(QUARTERS):
        block = piece[:, q * width : min(columns, (q + 1) * width)]
        if block.shape[1] < width:
            block = jnp.concatenate(
                [block, jnp.zeros((slots, width - block.shape[1]), block.dtype)], axis=1
            )
        term = dot(one_hot(hit & (((row >> 2) & 3) == q)), block)
        out = term if out is None else out + term
    out_ref[...] = out.astype(jnp.bfloat16)


def ahead_kernel(routes_ref, scores_ref, first_ref, gates_ref):
    slot = slots_of_tokens(routes_ref[...], lax.axis_index("g"), True)
    first_ref[...] = (slot >> 2) * CHUNK + (slot & 3)
    rows, tokens = gates_ref.shape[0], scores_ref.shape[1]
    sig = jax.nn.sigmoid(scores_ref[...])
    gates = ROUTE_SCALE * sig[:1] / jnp.sum(sig, axis=0, keepdims=True)
    owner = (lax.axis_index("g") * lax.axis_size("j") + lax.axis_index("j")) * CORES
    owner += lax.axis_index("k")
    mine = iota((rows, tokens), 1) == owner * rows + iota((rows, tokens), 0)
    gates_ref[...] = jnp.sum(jnp.where(mine, gates, 0.0), axis=1, keepdims=True)


def spread_kernel(first_ref, back_ref, out_ref):
    rows, width = back_ref.shape
    tokens, columns = out_ref.shape
    first = first_ref[...]
    row = iota((tokens, rows), 1)
    back = back_ref[...]
    for q in range(QUARTERS):
        stop = min(columns, (q + 1) * width)
        block = dot(one_hot(row == first + q * CAP), back[:, : stop - q * width])
        out_ref[:, q * width : stop] = block.astype(jnp.bfloat16)


def finish_kernel(gates_ref, parts_ref, out_ref):
    rows, model = out_ref.shape
    width = parts_ref.shape[1]
    gates = gates_ref[...]
    parts = parts_ref[...].astype(jnp.float32)
    per_group = parts.shape[0] // EXP_DP
    total = parts[:per_group]
    for group in range(1, EXP_DP):
        total = total + parts[group * per_group : (group + 1) * per_group]
    for part in range(per_group // rows):
        third, core = part // CORES, part % CORES
        base = min(third * CORES * width, model - CORES * width) + core * width
        skip = max(0, part * width - base) if core == 0 else 0
        block = total[part * rows : (part + 1) * rows, skip:] * gates
        out_ref[:, base + skip : base + width] = block.astype(jnp.bfloat16)


def call(kernel, shapes, in_specs, args, limit=VMEM_LIMIT, **more):
    single = not isinstance(shapes, list)
    return pl.pallas_call(
        kernel,
        out_shape=shapes,
        in_specs=in_specs,
        out_specs=VMEM if single else [VMEM] * len(shapes),
        compiler_params=pltpu.CompilerParams(vmem_limit_bytes=limit),
        **more,
    )(*args)


def in_hbm(x):
    return pltpu.with_memory_space_constraint(x, pltpu.HBM)


def exchange(x):
    return lax.ppermute(x, "k", [(0, 1), (1, 0)])


def over_dp(x):
    return lax.all_to_all(x, "dp", split_axis=0, concat_axis=0, tiled=True)


def per_device(tokens, scores, routes, w_gate, w_up, w_down):
    dp_count = lax.axis_size("dp")
    tok_rows, model = tokens.shape
    units = w_down.shape[0]
    thirds = lax.axis_size("j")
    owners = EXP_DP * thirds * CORES
    slots = dp_count * CAP
    half = model // CORES
    width = -(-model // (thirds * CORES * LANES)) * LANES
    quarter = -(-width // (QUARTERS * LANES)) * LANES
    bf, f32 = jnp.bfloat16, jnp.float32
    routes_row, scores_row = routes.reshape(1, tok_rows), scores.T

    def array(shape, dtype=bf):
        return jax.ShapeDtypeStruct(shape, dtype)

    flat = (dp_count * CHUNK, half // QUARTERS)
    outgoing = call(
        pick_kernel,
        array(flat),
        [HBM, HBM],
        (in_hbm(routes_row), in_hbm(tokens)),
        scratch_shapes=[
            pltpu.VMEM((1, tok_rows), jnp.int32),
            pltpu.VMEM((tok_rows, half), bf),
            pltpu.SemaphoreType.DMA((3,)),
        ],
    )
    arrived = over_dp(outgoing.reshape(dp_count, CHUNK, half // QUARTERS))
    *sent, kept = call(
        blocks_kernel,
        [array((units, CORES * width))] * (thirds - 1) + [pltpu.HBM((units, CORES * width), bf)],
        [HBM],
        (w_down,),
        scratch_shapes=[pltpu.SemaphoreType.DMA((thirds,))],
    )
    first, gates = call(
        ahead_kernel,
        [array((tok_rows, 1), jnp.int32), array((tok_rows // owners, 1), f32)],
        [VMEM] * 2,
        lax.optimization_barrier((routes_row, scores_row, sent))[:2],
    )
    w_up = call(
        stage_kernel,
        pltpu.VMEM(w_up.shape, bf),
        [HBM],
        (in_hbm(lax.optimization_barrier((w_up, sent))[0]),),
        scratch_shapes=[pltpu.SemaphoreType.DMA],
    )
    arrived = lax.optimization_barrier((arrived, sent, first, gates))[0]
    moved = [
        lax.ppermute(block, "j", [(i, (i + step) % thirds) for i in range(thirds)])
        for step, block in enumerate(sent, 1)
    ]
    other = exchange(arrived)

    partial = call(
        own_kernel,
        [array((slots, units), f32)] * 2,
        [VMEM] * 3,
        (arrived.reshape(flat), w_gate, w_up),
        cost_estimate=BESIDE,
    )
    hidden = call(
        hidden_kernel,
        array((slots, units)),
        [VMEM] * 5,
        (*partial, other.reshape(flat), w_gate, w_up),
    )
    all_hidden = lax.all_gather(hidden, "j", axis=0)
    mine, others = call(
        down_kernel,
        [array((slots, width), f32), array((slots, width))],
        [VMEM] * (1 + thirds),
        (all_hidden, *moved, kept),
    )
    piece = call(
        pack_kernel,
        array((dp_count * CHUNK, quarter)),
        [VMEM] * 2,
        (mine, lax.all_gather(others, "k", axis=0)),
    )
    back = over_dp(piece.reshape(dp_count, CHUNK, quarter))
    spread = call(
        spread_kernel,
        array((tok_rows, width)),
        [VMEM, VMEM],
        (first, back.reshape(dp_count * CHUNK, quarter)),
    )
    final = lax.all_to_all(
        spread.reshape(owners, tok_rows // owners, width),
        ("g", "j", "k"),
        split_axis=0,
        concat_axis=0,
        tiled=True,
    )
    return call(
        finish_kernel,
        array((tok_rows // owners, model)),
        [VMEM, VMEM],
        (gates, final.reshape(tok_rows, width)),
    )


def solution(mesh):
    dp_count, ctx_count = mesh.devices.shape
    split = Mesh(
        mesh.devices.reshape(dp_count, EXP_DP, ctx_count // EXP_DP // CORES, CORES),
        ("dp", "g", "j", "k"),
    )
    everywhere = ("dp", "g", "j", "k")
    in_specs = (
        P("dp", None),
        P("dp", None),
        P("dp", None),
        P(None, everywhere),
        P(None, everywhere),
        P(everywhere, None),
    )
    return jax.shard_map(
        per_device, mesh=split, in_specs=in_specs, out_specs=P(everywhere, None), check_vma=False
    )
```
